32 devices in a mesh: grp: 2 (over x), pair: 16 (over z, y, core).
Axes of the slice: x: 2, y: 2, z: 4, core: 2. Of those that a mesh axis runs over, the one named last changes fastest.
Arguments:
- three_center: bfloat16 [16, 3, 256, 4096], P('pair'), may hold values from -0.125 to 0.125
- block_mask: int32 [16, 3], P('pair'), may hold values 0 or 1
- green_occ: bfloat16 [16, 6, 4096], P('pair', 'grp'), parts along dimension 1, may hold values from -0.4375 to 0.4375
- green_virt: bfloat16 [16, 6, 4096], P('pair', 'grp'), parts along dimension 1, may hold values from -0.4375 to 0.4375
- green_mask: int32 [16, 3], P('pair'), may hold values 0 or 1
- block_of_slot: int32 [16], replicated, may hold values from 0 to 15, each once
Outputs:
- chi: float32 [256, 512], P('pair', 'grp'), parts along dimension 1
The draws below stay inside these ranges and needn't reach their ends.
There are 2 independent parts, one for each index of `grp`. The reference program is written for one: setup_inputs(seed, part) draws one part's arguments, and reference() takes and returns one part's arrays. A program takes and returns all parts, laid end to end along the dimension named above; an argument that names none is the same for every part. Nothing has to cross between parts.
Inputs may be any that keep to these rules, and one draw needn't show every extreme that they name: `block_of_slot`: every atom block stands in exactly one slot.
All inputs are finite; a program needn't handle non-finite values. No bound on the sum of `block_mask` or of `green_mask` on one device may be relied on, other than what follows from the above.
Results may differ from the reference program's by a relative error of at most 0.004.
Values may be sent and summed in bfloat16 or wider, within the bound.
A program may use at most 128 MiB of HBM per device.

```python
import jax
import jax.numpy as jnp
from jax import lax

BS = 64
PB = 256
HB = 1
HG = 1
KN = 3
KG = 3
NBLK = 16


def plant(values, key, low, largest):
    extent = values.shape
    place = [jax.random.randint(jax.random.fold_in(key, axis), (), 0, extent[axis]) for axis in range(len(extent))]
    values = values.at[tuple(place)].set(low)
    longest = extent.index(max(extent))
    place[longest] = (place[longest] + 1) % extent[longest]
    return values.at[tuple(place)].set(largest)


def levels(rng, dims, split, low, high):
    level = 1.0
    for axis_at, parts in split:
        draws = jax.random.uniform(jax.random.fold_in(jax.random.fold_in(rng, 6), axis_at), (parts,), jnp.float32, low / len(split), high / len(split))
        level = level * jnp.repeat(jnp.exp(draws), dims[axis_at] // parts).reshape((-1,) + (1,) * (len(dims) - 1 - axis_at))
    return level


def centred(key, dims, scale, bound, pieces=(), held_as=jnp.bfloat16):
    factor_of = levels(key, dims, pieces, -0.22, 0.18) if pieces else 1.0
    values = jax.random.normal(key, dims, jnp.float32) * scale * factor_of
    return jnp.minimum(jnp.maximum(values, -bound), bound).astype(held_as)


def setup_inputs(seed: int = 0, part: int = 0) -> dict:
    splits = jax.random.split(jax.random.key(seed), 7)
    part_keys = jax.random.split(jax.random.fold_in(splits[6], part), 7)
    return {
        "three_center": centred(splits[0], (NBLK, KN, PB, BS * BS), 2048 ** -0.5, 0.125, ((0, 16),)),
        "block_mask": plant((jax.random.randint(splits[1], (NBLK, KN), 0, 4) < 3).astype(jnp.int32), jax.random.fold_in(splits[1], 1), 0, 1),
        "green_occ": centred(part_keys[2], (NBLK, KG, BS * BS), (BS * KG) ** -0.5, 0.4375, ((0, 16),)),
        "green_virt": centred(part_keys[3], (NBLK, KG, BS * BS), (BS * KG) ** -0.5, 0.4375, ((0, 16),)),
        "green_mask": plant((jax.random.randint(splits[4], (NBLK, KG), 0, 4) < 3).astype(jnp.int32), jax.random.fold_in(splits[4], 1), 0, 1),
        "block_of_slot": jax.random.permutation(splits[5], NBLK).astype(jnp.int32),
    }


def invert(block_of_slot):
    amount = block_of_slot.shape[0]
    return jnp.zeros((amount,), jnp.int32).at[block_of_slot].set(jnp.arange(amount, dtype=jnp.int32))


def transform(blocks, gocc, gvirt):
    blocks_wide = blocks.astype(jnp.float32)
    lefts = []
    for target in range(-HB, HB + 1):
        running = jnp.zeros((blocks.shape[0], blocks.shape[2], BS, BS), jnp.float32)
        for middle in range(-HG, HG + 1):
            if abs(target - middle) <= HB:
                green_rows = jnp.roll(gocc[:, middle + HG], -(target - middle), axis=0)
                running = running + jnp.einsum('lij,lpjk->lpik', green_rows, blocks_wide[:, target - middle + HB])
        lefts.append(running.astype(jnp.bfloat16))
    left_wide = jnp.stack(lefts, axis=1).astype(jnp.float32)
    rights = []
    for target in range(-HB, HB + 1):
        running = jnp.zeros((blocks.shape[0], blocks.shape[2], BS, BS), jnp.float32)
        for middle in range(-HG, HG + 1):
            if abs(target - middle) <= HB:
                shifted = jnp.roll(left_wide[:, target - middle + HB], -middle, axis=0)
                running = running + jnp.einsum('lpij,ljk->lpik', shifted, gvirt[:, middle + HG])
        rights.append(running.astype(jnp.bfloat16))
    return jnp.stack(rights, axis=1)


def reference(three_center, block_mask, green_occ, green_virt, green_mask, block_of_slot):
    slot_of_block = invert(block_of_slot)
    masked = three_center * block_mask.astype(three_center.dtype)[:, :, None, None]
    green_keep = green_mask.astype(green_occ.dtype)[:, :, None]
    gocc = (green_occ * green_keep)[slot_of_block].reshape(NBLK, KG, BS, BS).astype(jnp.float32)
    gvirt = (green_virt * green_keep)[slot_of_block].reshape(NBLK, KG, BS, BS).astype(jnp.float32)
    curve = masked[slot_of_block]
    width = 32 if PB % 32 == 0 else PB
    stacked = jnp.moveaxis(curve.reshape(NBLK, KN, PB // width, width, BS, BS), 2, 0)
    right = lax.map(lambda piece: transform(piece, gocc, gvirt), stacked)
    right = jnp.moveaxis(right, 0, 2).reshape(NBLK, KN, PB, BS * BS)
    flat_tensor = jnp.moveaxis(curve, 2, 0).reshape(PB, -1)
    flat_right = jnp.moveaxis(right, 2, 0).reshape(PB, -1)
    return jnp.dot(flat_tensor, flat_right.T, preferred_element_type=jnp.float32)
```

```python
import functools

import jax
import jax.numpy as jnp
from jax import lax
from jax.experimental import pallas as pl
from jax.experimental.pallas import tpu as pltpu
from jax.sharding import PartitionSpec as P

BS = 64
HB = 1
HG = 1
KN = 3
KG = 3
MESH = pl.DeviceIdType.MESH


def invert(block_of_slot):
    amount = block_of_slot.shape[0]
    return (
        jnp.zeros((amount,), jnp.int32).at[block_of_slot].set(jnp.arange(amount, dtype=jnp.int32))
    )


def build_left(blocks, columns, gocc, block_count):
    lefts = []
    for target in range(-HB, HB + 1):
        middles = [m for m in range(HG, -HG - 1, -1) if abs(target - m) <= HB]
        green_cat = jnp.concatenate(
            [gocc[(columns + (target - m)) % block_count, m + HG] for m in middles], axis=2
        )
        lowest = target - middles[0] + HB
        tensor_cat = blocks[:, lowest : lowest + len(middles)]
        tensor_cat = tensor_cat.reshape(blocks.shape[0], len(middles) * BS, blocks.shape[3])
        lefts.append(
            jnp.einsum(
                "lij,ljq->liq", green_cat, tensor_cat, preferred_element_type=jnp.float32
            ).astype(jnp.bfloat16)
        )
    return jnp.stack(lefts, axis=1)


def build_right(left_turned, gvirt):
    rights = []
    count = left_turned.shape[0]
    for target in range(-HB, HB + 1):
        middles = [m for m in range(-HG, HG + 1) if abs(target - m) <= HB]
        virt_cat = gvirt[:, middles[0] + HG : middles[-1] + HG + 1].reshape(
            count, len(middles) * BS, BS
        )
        left_cat = jnp.concatenate(
            [jnp.roll(left_turned[:, target - m + HB], -m, axis=0) for m in middles], axis=1
        )
        rights.append(
            jnp.einsum(
                "ljk,ljq->lkq", virt_cat, left_cat, preferred_element_type=jnp.float32
            ).astype(jnp.bfloat16)
        )
    return jnp.stack(rights, axis=1)


def on_device(three_center, block_mask, green_occ, green_virt, green_mask, block_of_slot):
    aux_count = three_center.shape[2]
    block_count = block_of_slot.shape[0]
    local_aux = aux_count // lax.axis_size("pair")
    slot_of_block = invert(block_of_slot)
    masked = three_center * block_mask.astype(jnp.bfloat16)[:, :, None, None]
    green_keep = green_mask.astype(jnp.bfloat16)[:, :, None]
    every_occ, every_virt = (
        lax.all_gather(green_occ * green_keep, "pair", axis=0, tiled=True),
        lax.all_gather(green_virt * green_keep, "pair", axis=0, tiled=True),
    )
    gocc = every_occ[slot_of_block].reshape(block_count, KG, BS, BS)
    gvirt = every_virt[slot_of_block].reshape(block_count, KG, BS, BS)
    regrouped = lax.all_to_all(masked, "pair", split_axis=2, concat_axis=0, tiled=True)
    curve = regrouped[slot_of_block].reshape(block_count, KN, local_aux, BS, BS)
    curve = curve.transpose(0, 1, 3, 2, 4).reshape(block_count, KN, BS, local_aux * BS)
    left = build_left(curve, jnp.arange(block_count, dtype=jnp.int32), gocc, block_count)
    left = left.reshape(block_count, KN, BS, local_aux, BS)
    left_turned = left.transpose(0, 1, 4, 3, 2).reshape(block_count, KN, BS, local_aux * BS)
    right_turned = build_right(left_turned, gvirt)
    right = right_turned.reshape(block_count, KN, BS, local_aux, BS).transpose(0, 1, 3, 4, 2)
    right_slots = right.reshape(block_count, KN, local_aux, BS * BS)[block_of_slot]
    returned = lax.all_to_all(right_slots, "pair", split_axis=0, concat_axis=2, tiled=True)
    return lax.psum_scatter(
        lax.dot_general(
            masked, returned, (((0, 1, 3), (0, 1, 3)), ((), ())), preferred_element_type=jnp.float32
        ),
        "pair",
        scatter_dimension=0,
        tiled=True,
    )


def row_sliced(n):
    return BS % n == 0 and (BS // n) * BS % 128 == 0


def greet(n, me):
    barrier = pltpu.get_barrier_semaphore()

    def hello(k, carry):
        pl.semaphore_signal(
            barrier, inc=1, device_id={"pair": lax.rem(me + k, n)}, device_id_type=MESH
        )
        return carry

    lax.fori_loop(1, n, hello, 0)
    pl.semaphore_wait(barrier, n - 1)


def gather_kernel(n, own_ref, every_ref, send_sem, recv_sem, local_sem):
    me = lax.axis_index("pair")
    greet(n, me)
    local = pltpu.make_async_copy(own_ref, every_ref.at[me], local_sem)
    local.start()

    def send_of(k):
        return pltpu.make_async_remote_copy(
            src_ref=own_ref,
            dst_ref=every_ref.at[me],
            send_sem=send_sem.at[k],
            recv_sem=recv_sem.at[k],
            device_id={"pair": lax.rem(me + k, n)},
            device_id_type=MESH,
        )

    def start(k, carry):
        send_of(k).start()
        return carry

    def finish(k, carry):
        copy = send_of(k)
        copy.wait_recv()
        copy.wait_send()
        return carry

    lax.fori_loop(1, n, start, 0)
    lax.fori_loop(1, n, finish, 0)
    local.wait()


def gather_small(own, n):
    return pl.pallas_call(
        functools.partial(gather_kernel, n),
        out_shape=jax.ShapeDtypeStruct((n,) + own.shape, own.dtype),
        in_specs=[pl.BlockSpec(memory_space=pltpu.VMEM)],
        out_specs=pl.BlockSpec(memory_space=pltpu.VMEM),
        scratch_shapes=[
            pltpu.SemaphoreType.DMA((n,)),
            pltpu.SemaphoreType.DMA((n,)),
            pltpu.SemaphoreType.DMA,
        ],
        compiler_params=pltpu.CompilerParams(collective_id=0, has_side_effects=True),
        name="gather_greens",
    )(own)


def scatter_kernel(n, part_ref, out_ref, landed, send_sem, recv_sem):
    me = lax.axis_index("pair")
    rows = out_ref.shape[0]
    greet(n, me)

    def send_of(k):
        to = lax.rem(me + k, n)
        return pltpu.make_async_remote_copy(
            src_ref=part_ref.at[pl.ds(pl.multiple_of(to * rows, rows), rows)],
            dst_ref=landed.at[k],
            send_sem=send_sem.at[k],
            recv_sem=recv_sem.at[k],
            device_id={"pair": to},
            device_id_type=MESH,
        )

    def start(k, carry):
        send_of(k).start()
        return carry

    def finish(k, carry):
        copy = send_of(k)
        copy.wait_recv()
        copy.wait_send()
        return carry

    lax.fori_loop(1, n, start, 0)
    lax.fori_loop(1, n, finish, 0)
    total = part_ref[pl.ds(pl.multiple_of(me * rows, rows), rows), :]
    for k in range(1, n):
        total = total + landed[k]
    out_ref[...] = total


def scatter_sum(part, n):
    rows = part.shape[0] // n
    return pl.pallas_call(
        functools.partial(scatter_kernel, n),
        out_shape=jax.ShapeDtypeStruct((rows, part.shape[1]), jnp.float32),
        in_specs=[pl.BlockSpec(memory_space=pltpu.VMEM)],
        out_specs=pl.BlockSpec(memory_space=pltpu.VMEM),
        scratch_shapes=[
            pltpu.VMEM((n, rows, part.shape[1]), jnp.float32),
            pltpu.SemaphoreType.DMA((n,)),
            pltpu.SemaphoreType.DMA((n,)),
        ],
        compiler_params=pltpu.CompilerParams(collective_id=1, has_side_effects=True),
        name="scatter_chi",
    )(part)


def swap_major(chunks):
    return jnp.swapaxes(jnp.stack(chunks, axis=0), 0, 1)


def left_kernel(green_ref, tensor_ref, left_ref):
    count = tensor_ref.shape[2]
    half = count // 2
    pairs = BS * BS // 128
    low = lax.broadcasted_iota(jnp.int32, (half, pairs, 128), 2) < BS
    rows = []
    for a in range(KN):
        x = swap_major([tensor_ref[0, a, :, 128 * t : 128 * (t + 1)] for t in range(pairs)])
        first, second = x[:half], x[half:]
        even = jnp.where(low, first, pltpu.roll(second, BS, 2))
        odd = jnp.where(low, pltpu.roll(first, BS, 2), second)
        for y in (even, odd):
            rows.append(jnp.concatenate([y[p] for p in range(half)], axis=1))
    stacked = jnp.concatenate(rows, axis=0)
    result = jnp.dot(green_ref[...], stacked, preferred_element_type=jnp.float32)
    result = result.astype(jnp.bfloat16)
    for a in range(KN):
        base = a * BS
        even = jnp.stack(
            [result[base : base + pairs, 128 * p : 128 * (p + 1)] for p in range(half)], axis=0
        )
        odd = jnp.stack(
            [result[base + pairs : base + BS, 128 * p : 128 * (p + 1)] for p in range(half)],
            axis=0,
        )
        first = jnp.where(low, even, pltpu.roll(odd, BS, 2))
        second = jnp.where(low, pltpu.roll(even, BS, 2), odd)
        back = jnp.swapaxes(jnp.concatenate([first, second], axis=0), 0, 1)
        for t in range(pairs):
            left_ref[0, a, :, 128 * t : 128 * (t + 1)] = back[t]


def left_products(tensor, green, chunk=32):
    aux = tensor.shape[2]
    spec = pl.BlockSpec((1, KN, chunk, BS * BS), lambda q: (0, 0, q, 0))
    return pl.pallas_call(
        left_kernel,
        grid=(aux // chunk,),
        out_shape=jax.ShapeDtypeStruct(tensor.shape, jnp.bfloat16),
        in_specs=[pl.BlockSpec((KN * BS, KN * BS), lambda q: (0, 0)), spec],
        out_specs=spec,
        compiler_params=pltpu.CompilerParams(vmem_limit_bytes=48 * 1024 * 1024),
        cost_estimate=pl.CostEstimate(
            flops=2 * 9 * BS * BS * BS * aux,
            bytes_accessed=4 * KN * aux * BS * BS,
            transcendentals=0,
        ),
        name="left_products",
    )(green, tensor)


def chi_kernel(slot_ref, mask_ref, before_ref, here_ref, after_ref, tensor_ref, virt_ref, chi_ref):
    lam = pl.program_id(0)
    width = tensor_ref.shape[3]
    rows = width // BS
    lefts = (before_ref, here_ref, after_ref)
    line = lax.broadcasted_iota(jnp.int32, (width, width), 0) // BS
    column = lax.broadcasted_iota(jnp.int32, (width, width), 1) // BS
    spread = []
    for c in range(KG):
        block = jnp.concatenate([virt_ref[0, c]] * rows, axis=1)
        block = jnp.concatenate([block] * rows, axis=0)
        spread.append(jnp.where(line == column, block, jnp.zeros_like(block)))
    total = jnp.zeros(chi_ref.shape, jnp.float32)
    for a in range(-HB, HB + 1):
        right = jnp.zeros((tensor_ref.shape[2], width), jnp.float32)
        for c in range(-HG, HG + 1):
            if abs(a - c) <= HB:
                right = right + jnp.dot(
                    lefts[c + HG][0, a - c + HB],
                    spread[c + HG],
                    preferred_element_type=jnp.float32,
                )
        keep = mask_ref[slot_ref[lam] * KN + a + HB].astype(jnp.float32)
        right = (right * keep).astype(jnp.bfloat16)
        total = total + lax.dot_general(
            tensor_ref[0, a + HB],
            right,
            (((1,), (1,)), ((), ())),
            preferred_element_type=jnp.float32,
        )

    @pl.when(lam == 0)
    def _():
        chi_ref[...] = total

    @pl.when(lam != 0)
    def _():
        chi_ref[...] += total


def chi_partial(slot_of_block, every_mask, left, tensor, virt):
    n, _, aux, width = tensor.shape

    def at(shift):
        return pl.BlockSpec(
            (1, KN, aux, width),
            lambda lam, slot, mask: (slot[lax.rem(lam + shift + n, n)], 0, 0, 0),
        )

    return pl.pallas_call(
        chi_kernel,
        grid_spec=pltpu.PrefetchScalarGridSpec(
            num_scalar_prefetch=2,
            grid=(n,),
            in_specs=[
                at(-1),
                at(0),
                at(1),
                at(0),
                pl.BlockSpec((1, KG, BS, BS), lambda lam, slot, mask: (slot[lam], 0, 0, 0)),
            ],
            out_specs=pl.BlockSpec((aux, aux), lambda lam, slot, mask: (0, 0)),
        ),
        out_shape=jax.ShapeDtypeStruct((aux, aux), jnp.float32),
        compiler_params=pltpu.CompilerParams(vmem_limit_bytes=48 * 1024 * 1024),
        cost_estimate=pl.CostEstimate(
            flops=2 * n * aux * width * (7 * width + KN * aux),
            bytes_accessed=8 * n * KN * aux * width,
            transcendentals=0,
        ),
        name="chi_partial",
    )(slot_of_block, every_mask, left, left, left, tensor, virt)


def green_matrix(gocc, every_mask, slot_of_block, column):
    n = slot_of_block.shape[0]
    keep = every_mask[slot_of_block[column]].astype(jnp.bfloat16)
    zero = jnp.zeros((BS, BS), jnp.bfloat16)
    lines = []
    for target in range(-HB, HB + 1):
        line = []
        for source in range(-HB, HB + 1):
            step = target - source
            if abs(step) <= HG:
                slot = slot_of_block[(column + source + n) % n]
                line.append(gocc[slot, step + HG] * keep[source + HB])
            else:
                line.append(zero)
        lines.append(jnp.concatenate(line, axis=1))
    whole = jnp.concatenate(lines, axis=0).reshape(KN, BS // 2, 2, KN, BS // 2, 2)
    return whole.transpose(0, 2, 1, 3, 5, 4).reshape(KN * BS, KN * BS)


def by_rows(array, n):
    _, blocks, aux, cells = array.shape
    moved = lax.all_to_all(array, "pair", split_axis=3, concat_axis=0, tiled=True)
    return moved.reshape(n, blocks, aux, cells // n)


def by_row_slices(three_center, block_mask, green_occ, green_virt, green_mask, block_of_slot):
    n = lax.axis_size("pair")
    slot_of_block = invert(block_of_slot)
    green_keep = green_mask.astype(jnp.bfloat16)[:, :, None]
    greens = jnp.concatenate([green_occ * green_keep, green_virt * green_keep], axis=1)
    greens = greens.reshape(16, 2 * KG * BS * BS // 16)
    mask = jnp.zeros((16, 128), jnp.bfloat16).at[0, :KN].set(block_mask[0].astype(jnp.bfloat16))
    every = gather_small(jnp.concatenate([greens, mask], axis=1), n)
    tensor_rows = by_rows(three_center, n)
    every_mask = every[:, 0, greens.shape[1] : greens.shape[1] + KN].astype(jnp.int32)
    every_green = every[:, :, : greens.shape[1]].reshape(n, 2, KG, BS, BS)
    column = block_of_slot[lax.axis_index("pair")]
    green = green_matrix(every_green[:, 0], every_mask, slot_of_block, column)
    left = left_products(three_center, green)
    left_rows = by_rows(left, n)
    part = chi_partial(
        slot_of_block, every_mask.reshape(-1), left_rows, tensor_rows, every_green[:, 1]
    )
    return scatter_sum(part, n)


def solution(mesh):
    return jax.shard_map(
        by_row_slices if row_sliced(mesh.shape["pair"]) else on_device,
        mesh=mesh,
        in_specs=(
            P("pair", None, None, None),
            P("pair", None),
            P("pair", "grp", None),
            P("pair", "grp", None),
            P("pair", None),
            P(),
        ),
        out_specs=P("pair", "grp"),
        check_vma=False,
    )
```

```python
import functools

import jax
import jax.numpy as jnp
from jax import lax
from jax.experimental import pallas as pl
from jax.experimental.pallas import tpu as pltpu
from jax.sharding import PartitionSpec as P

BS = 64
HB = 1
HG = 1
KN = 3
KG = 3
MESH = pl.DeviceIdType.MESH


def invert(block_of_slot):
    amount = block_of_slot.shape[0]
    return (
        jnp.zeros((amount,), jnp.int32).at[block_of_slot].set(jnp.arange(amount, dtype=jnp.int32))
    )


def build_left(blocks, columns, gocc, block_count):
    lefts = []
    for target in range(-HB, HB + 1):
        middles = [m for m in range(HG, -HG - 1, -1) if abs(target - m) <= HB]
        green_cat = jnp.concatenate(
            [gocc[(columns + (target - m)) % block_count, m + HG] for m in middles], axis=2
        )
        lowest = target - middles[0] + HB
        tensor_cat = blocks[:, lowest : lowest + len(middles)]
        tensor_cat = tensor_cat.reshape(blocks.shape[0], len(middles) * BS, blocks.shape[3])
        lefts.append(
            jnp.einsum(
                "lij,ljq->liq", green_cat, tensor_cat, preferred_element_type=jnp.float32
            ).astype(jnp.bfloat16)
        )
    return jnp.stack(lefts, axis=1)


def build_right(left_turned, gvirt):
    rights = []
    count = left_turned.shape[0]
    for target in range(-HB, HB + 1):
        middles = [m for m in range(-HG, HG + 1) if abs(target - m) <= HB]
        virt_cat = gvirt[:, middles[0] + HG : middles[-1] + HG + 1].reshape(
            count, len(middles) * BS, BS
        )
        left_cat = jnp.concatenate(
            [jnp.roll(left_turned[:, target - m + HB], -m, axis=0) for m in middles], axis=1
        )
        rights.append(
            jnp.einsum(
                "ljk,ljq->lkq", virt_cat, left_cat, preferred_element_type=jnp.float32
            ).astype(jnp.bfloat16)
        )
    return jnp.stack(rights, axis=1)


def on_device(three_center, block_mask, green_occ, green_virt, green_mask, block_of_slot):
    aux_count = three_center.shape[2]
    block_count = block_of_slot.shape[0]
    local_aux = aux_count // lax.axis_size("pair")
    slot_of_block = invert(block_of_slot)
    masked = three_center * block_mask.astype(jnp.bfloat16)[:, :, None, None]
    green_keep = green_mask.astype(jnp.bfloat16)[:, :, None]
    every_occ, every_virt = (
        lax.all_gather(green_occ * green_keep, "pair", axis=0, tiled=True),
        lax.all_gather(green_virt * green_keep, "pair", axis=0, tiled=True),
    )
    gocc = every_occ[slot_of_block].reshape(block_count, KG, BS, BS)
    gvirt = every_virt[slot_of_block].reshape(block_count, KG, BS, BS)
    regrouped = lax.all_to_all(masked, "pair", split_axis=2, concat_axis=0, tiled=True)
    curve = regrouped[slot_of_block].reshape(block_count, KN, local_aux, BS, BS)
    curve = curve.transpose(0, 1, 3, 2, 4).reshape(block_count, KN, BS, local_aux * BS)
    left = build_left(curve, jnp.arange(block_count, dtype=jnp.int32), gocc, block_count)
    left = left.reshape(block_count, KN, BS, local_aux, BS)
    left_turned = left.transpose(0, 1, 4, 3, 2).reshape(block_count, KN, BS, local_aux * BS)
    right_turned = build_right(left_turned, gvirt)
    right = right_turned.reshape(block_count, KN, BS, local_aux, BS).transpose(0, 1, 3, 4, 2)
    right_slots = right.reshape(block_count, KN, local_aux, BS * BS)[block_of_slot]
    returned = lax.all_to_all(right_slots, "pair", split_axis=0, concat_axis=2, tiled=True)
    return lax.psum_scatter(
        lax.dot_general(
            masked, returned, (((0, 1, 3), (0, 1, 3)), ((), ())), preferred_element_type=jnp.float32
        ),
        "pair",
        scatter_dimension=0,
        tiled=True,
    )


def row_sliced(shape):
    n = shape["pair"]
    return shape["grp"] == 2 and BS % n == 0 and (BS // n) * BS % 128 == 0


def greet(n, me):
    barrier = pltpu.get_barrier_semaphore()

    def hello(k, carry):
        pl.semaphore_signal(
            barrier, inc=1, device_id={"pair": lax.rem(me + k, n)}, device_id_type=MESH
        )
        return carry

    lax.fori_loop(1, n, hello, 0)
    pl.semaphore_signal(
        barrier, inc=1, device_id={"grp": 1 - lax.axis_index("grp")}, device_id_type=MESH
    )
    pl.semaphore_wait(barrier, n)


def swap_major(chunks):
    return jnp.swapaxes(jnp.stack(chunks, axis=0), 0, 1)


def left_chunk(green_ref, tensor_ref, left_ref, rows_at, count):
    half = count // 2
    pairs = BS * BS // 128
    at = pl.ds(rows_at, count)
    low = lax.broadcasted_iota(jnp.int32, (half, pairs, 128), 2) < BS
    rows = []
    for a in range(KN):
        x = swap_major([tensor_ref[0, a, at, 128 * t : 128 * (t + 1)] for t in range(pairs)])
        first, second = x[:half], x[half:]
        even = jnp.where(low, first, pltpu.roll(second, BS, 2))
        odd = jnp.where(low, pltpu.roll(first, BS, 2), second)
        for y in (even, odd):
            rows.append(jnp.concatenate([y[p] for p in range(half)], axis=1))
    stacked = jnp.concatenate(rows, axis=0)
    result = jnp.dot(green_ref[...], stacked, preferred_element_type=jnp.float32)
    result = result.astype(jnp.bfloat16)
    for a in range(KN):
        base = a * BS
        even = jnp.stack(
            [result[base : base + pairs, 128 * p : 128 * (p + 1)] for p in range(half)], axis=0
        )
        odd = jnp.stack(
            [result[base + pairs : base + BS, 128 * p : 128 * (p + 1)] for p in range(half)],
            axis=0,
        )
        first = jnp.where(low, even, pltpu.roll(odd, BS, 2))
        second = jnp.where(low, pltpu.roll(even, BS, 2), odd)
        back = jnp.swapaxes(jnp.concatenate([first, second], axis=0), 0, 1)
        for t in range(pairs):
            left_ref[a, at, 128 * t : 128 * (t + 1)] = back[t]


def fill_green(n, column, slots_ref, pack_ref, every_ref, green_ref):
    keep_row = KG * BS
    for target in range(-HB, HB + 1):
        line = []
        for source in range(-HB, HB + 1):
            step = target - source
            if abs(step) <= HG:
                slot = slots_ref[lax.rem(column + source + n, n)]
                at = (step + HG) * BS
                block = every_ref[slot, at : at + BS, :][:, :BS].astype(jnp.float32)
                keep = pack_ref[keep_row : keep_row + 16, :][:1, source + HB : source + HB + 1]
                line.append((block * keep.astype(jnp.float32)).astype(jnp.bfloat16))
            else:
                line.append(jnp.zeros((BS, BS), jnp.bfloat16))
        at = (target + HB) * BS
        green_ref[at : at + BS, :] = jnp.concatenate(line, axis=1)


def chi_of_block(n, lam, slots_ref, every_ref, left_rows, tensor_rows, part_ref):
    aux, width = tensor_rows.shape[2:]
    rows = width // BS
    here = slots_ref[lam]
    line = lax.broadcasted_iota(jnp.int32, (width, width), 0) // BS
    column = lax.broadcasted_iota(jnp.int32, (width, width), 1) // BS
    spread = []
    for c in range(KG):
        block = every_ref[here, c * BS : (c + 1) * BS, :][:, BS : 2 * BS]
        block = jnp.concatenate([block] * rows, axis=1)
        block = jnp.concatenate([block] * rows, axis=0)
        spread.append(jnp.where(line == column, block, jnp.zeros_like(block)))
    keeps = every_ref[here, KG * BS : KG * BS + 16, :][:1].astype(jnp.float32)
    total = part_ref[...]
    for a in range(-HB, HB + 1):
        right = jnp.zeros((aux, width), jnp.float32)
        for c in range(-HG, HG + 1):
            if abs(a - c) <= HB:
                slot = slots_ref[lax.rem(lam + c + n, n)]
                right = right + jnp.dot(
                    left_rows[slot, a - c + HB],
                    spread[c + HG],
                    preferred_element_type=jnp.float32,
                )
        right = (right * keeps[:, a + HB : a + HB + 1]).astype(jnp.bfloat16)
        total = total + lax.dot_general(
            tensor_rows[here, a + HB],
            right,
            (((1,), (1,)), ((), ())),
            preferred_element_type=jnp.float32,
        )
    part_ref[...] = total


def whole_kernel(
    n, chunk, blocks_ref, slots_ref, pack_ref, tensor_ref, out_ref,
    every, green, left, left_rows, tensor_rows, part, landed,
    pack_send, pack_recv, tensor_send, tensor_recv, pass_send, pass_recv,
    left_send, left_recv, chi_send, chi_recv, own_sem,
):
    me = lax.axis_index("pair")
    grp = lax.axis_index("grp")
    aux = tensor_ref.shape[2]
    width = tensor_rows.shape[3]
    chunks = aux // chunk
    out_rows = aux // n
    share = pl.ds(pl.multiple_of(grp * (aux // 2), aux // 2), aux // 2)
    mine = pl.ds(pl.multiple_of(me * width, width), width)

    def lanes(to):
        return pl.ds(pl.multiple_of(to * width, width), width)

    def remote(src, dst, send, recv, target):
        return pltpu.make_async_remote_copy(
            src_ref=src, dst_ref=dst, send_sem=send, recv_sem=recv,
            device_id=target, device_id_type=MESH,
        )

    def pack_copy(k):
        to = lax.rem(me + k, n)
        return remote(pack_ref, every.at[me], pack_send.at[k], pack_recv.at[k], {"pair": to})

    def tensor_copy(k):
        to = lax.rem(me + k, n)
        return remote(
            tensor_ref.at[0, :, share, lanes(to)], tensor_rows.at[me, :, share, :],
            tensor_send.at[k], tensor_recv.at[k], {"pair": to},
        )

    def pass_copy(k):
        source = lax.rem(me - k + n, n)
        where = tensor_rows.at[source, :, share, :]
        return remote(where, where, pass_send.at[k], pass_recv.at[k], {"grp": 1 - grp})

    def left_copy(q, k):
        to = lax.rem(me + k, n)
        at = pl.ds(pl.multiple_of(q * chunk, chunk), chunk)
        return remote(
            left.at[:, at, lanes(to)], left_rows.at[me, :, at, :],
            left_send.at[q, k], left_recv.at[q, k], {"pair": to},
        )

    def chi_copy(k):
        to = lax.rem(me + k, n)
        return remote(
            part.at[pl.ds(pl.multiple_of(to * out_rows, out_rows), out_rows)], landed.at[k],
            chi_send.at[k], chi_recv.at[k], {"pair": to},
        )

    def each(act, low=1):
        def body(k, carry):
            act(k)
            return carry

        lax.fori_loop(low, n, body, 0)

    greet(n, me)
    each(lambda k: pack_copy(k).start())
    each(lambda k: tensor_copy(k).start())
    own_pack = pltpu.make_async_copy(pack_ref, every.at[me], own_sem.at[0])
    own_tensor = pltpu.make_async_copy(
        tensor_ref.at[0, :, :, mine], tensor_rows.at[me], own_sem.at[1]
    )
    own_pack.start()
    own_tensor.start()
    own_pack.wait()
    each(lambda k: pack_copy(k).wait_recv())
    fill_green(n, blocks_ref[me], slots_ref, pack_ref, every, green)

    def make_left(q, carry):
        left_chunk(green, tensor_ref, left, pl.multiple_of(q * chunk, chunk), chunk)
        each(lambda k: left_copy(q, k).start())
        return carry

    lax.fori_loop(0, chunks, make_left, 0)
    own_left = pltpu.make_async_copy(left.at[:, :, mine], left_rows.at[me], own_sem.at[2])
    own_left.start()

    def hand_on(k):
        tensor_copy(k).wait_recv()
        pass_copy(k).start()

    each(hand_on)
    part[...] = jnp.zeros_like(part)
    own_tensor.wait()
    own_left.wait()

    def left_all(k):
        def body(q, carry):
            left_copy(q, k).wait_recv()
            return carry

        lax.fori_loop(0, chunks, body, 0)

    each(lambda k: pass_copy(k).wait_recv())
    each(left_all)

    def add_block(lam, carry):
        chi_of_block(n, lam, slots_ref, every, left_rows, tensor_rows, part)
        return carry

    lax.fori_loop(0, n, add_block, 0)
    each(lambda k: chi_copy(k).start())

    def sent(k):
        pack_copy(k).wait_send()
        tensor_copy(k).wait_send()
        pass_copy(k).wait_send()

        def body(q, carry):
            left_copy(q, k).wait_send()
            return carry

        lax.fori_loop(0, chunks, body, 0)

    each(sent)
    each(lambda k: chi_copy(k).wait_recv())
    total = part[pl.ds(pl.multiple_of(me * out_rows, out_rows), out_rows), :]
    for k in range(1, n):
        total = total + landed[k]
    out_ref[...] = total
    each(lambda k: chi_copy(k).wait_send())


def by_row_slices(three_center, block_mask, green_occ, green_virt, green_mask, block_of_slot):
    n = lax.axis_size("pair")
    aux = three_center.shape[2]
    width = BS * BS // n
    chunk = 32
    slot_of_block = invert(block_of_slot)
    keep = green_mask.astype(jnp.bfloat16)[0, :, None, None]
    occ = green_occ.reshape(KG, BS // 2, 2, BS // 2, 2).transpose(0, 2, 1, 4, 3)
    occ = occ.reshape(KG, BS, BS)
    virt = green_virt.reshape(KG, BS, BS)
    greens = (jnp.concatenate([occ, virt], axis=2) * keep).reshape(KG * BS, 2 * BS)
    mask = jnp.pad(block_mask.astype(jnp.bfloat16), ((0, 15), (0, 2 * BS - KN)))
    pack = jnp.concatenate([greens, mask], axis=0)
    smem = pl.BlockSpec(memory_space=pltpu.SMEM)
    vmem = pl.BlockSpec(memory_space=pltpu.VMEM)
    sems = pltpu.SemaphoreType.DMA
    return pl.pallas_call(
        functools.partial(whole_kernel, n, chunk),
        out_shape=jax.ShapeDtypeStruct((aux // n, aux), jnp.float32),
        in_specs=[smem, smem, vmem, vmem],
        out_specs=vmem,
        scratch_shapes=[
            pltpu.VMEM((n,) + pack.shape, jnp.bfloat16),
            pltpu.VMEM((KN * BS, KN * BS), jnp.bfloat16),
            pltpu.VMEM((KN, aux, BS * BS), jnp.bfloat16),
            pltpu.VMEM((n, KN, aux, width), jnp.bfloat16),
            pltpu.VMEM((n, KN, aux, width), jnp.bfloat16),
            pltpu.VMEM((aux, aux), jnp.float32),
            pltpu.VMEM((n, aux // n, aux), jnp.float32),
            sems((n,)), sems((n,)), sems((n,)), sems((n,)), sems((n,)), sems((n,)),
            sems((aux // chunk, n)), sems((aux // chunk, n)), sems((n,)), sems((n,)), sems((3,)),
        ],
        compiler_params=pltpu.CompilerParams(
            collective_id=0, has_side_effects=True, vmem_limit_bytes=48 * 1024 * 1024
        ),
        name="polarizability",
    )(block_of_slot, slot_of_block, pack, three_center)


def solution(mesh):
    return jax.shard_map(
        by_row_slices if row_sliced(mesh.shape) else on_device,
        mesh=mesh,
        in_specs=(
            P("pair", None, None, None),
            P("pair", None),
            P("pair", "grp", None),
            P("pair", "grp", None),
            P("pair", None),
            P(),
        ),
        out_specs=P("pair", "grp"),
        check_vma=False,
    )
```

```python
import functools

import jax
import jax.numpy as jnp
from jax import lax
from jax.experimental import pallas as pl
from jax.experimental.pallas import tpu as pltpu
from jax.sharding import PartitionSpec as P

BS = 64
HB = 1
HG = 1
KN = 3
KG = 3
MESH = pl.DeviceIdType.MESH


def invert(block_of_slot):
    amount = block_of_slot.shape[0]
    return (
        jnp.zeros((amount,), jnp.int32).at[block_of_slot].set(jnp.arange(amount, dtype=jnp.int32))
    )


def build_left(blocks, columns, gocc, block_count):
    lefts = []
    for target in range(-HB, HB + 1):
        middles = [m for m in range(HG, -HG - 1, -1) if abs(target - m) <= HB]
        green_cat = jnp.concatenate(
            [gocc[(columns + (target - m)) % block_count, m + HG] for m in middles], axis=2
        )
        lowest = target - middles[0] + HB
        tensor_cat = blocks[:, lowest : lowest + len(middles)]
        tensor_cat = tensor_cat.reshape(blocks.shape[0], len(middles) * BS, blocks.shape[3])
        lefts.append(
            jnp.einsum(
                "lij,ljq->liq", green_cat, tensor_cat, preferred_element_type=jnp.float32
            ).astype(jnp.bfloat16)
        )
    return jnp.stack(lefts, axis=1)


def build_right(left_turned, gvirt):
    rights = []
    count = left_turned.shape[0]
    for target in range(-HB, HB + 1):
        middles = [m for m in range(-HG, HG + 1) if abs(target - m) <= HB]
        virt_cat = gvirt[:, middles[0] + HG : middles[-1] + HG + 1].reshape(
            count, len(middles) * BS, BS
        )
        left_cat = jnp.concatenate(
            [jnp.roll(left_turned[:, target - m + HB], -m, axis=0) for m in middles], axis=1
        )
        rights.append(
            jnp.einsum(
                "ljk,ljq->lkq", virt_cat, left_cat, preferred_element_type=jnp.float32
            ).astype(jnp.bfloat16)
        )
    return jnp.stack(rights, axis=1)


def on_device(three_center, block_mask, green_occ, green_virt, green_mask, block_of_slot):
    aux_count = three_center.shape[2]
    block_count = block_of_slot.shape[0]
    local_aux = aux_count // lax.axis_size("pair")
    slot_of_block = invert(block_of_slot)
    masked = three_center * block_mask.astype(jnp.bfloat16)[:, :, None, None]
    green_keep = green_mask.astype(jnp.bfloat16)[:, :, None]
    every_occ, every_virt = (
        lax.all_gather(green_occ * green_keep, "pair", axis=0, tiled=True),
        lax.all_gather(green_virt * green_keep, "pair", axis=0, tiled=True),
    )
    gocc = every_occ[slot_of_block].reshape(block_count, KG, BS, BS)
    gvirt = every_virt[slot_of_block].reshape(block_count, KG, BS, BS)
    regrouped = lax.all_to_all(masked, "pair", split_axis=2, concat_axis=0, tiled=True)
    curve = regrouped[slot_of_block].reshape(block_count, KN, local_aux, BS, BS)
    curve = curve.transpose(0, 1, 3, 2, 4).reshape(block_count, KN, BS, local_aux * BS)
    left = build_left(curve, jnp.arange(block_count, dtype=jnp.int32), gocc, block_count)
    left = left.reshape(block_count, KN, BS, local_aux, BS)
    left_turned = left.transpose(0, 1, 4, 3, 2).reshape(block_count, KN, BS, local_aux * BS)
    right_turned = build_right(left_turned, gvirt)
    right = right_turned.reshape(block_count, KN, BS, local_aux, BS).transpose(0, 1, 3, 4, 2)
    right_slots = right.reshape(block_count, KN, local_aux, BS * BS)[block_of_slot]
    returned = lax.all_to_all(right_slots, "pair", split_axis=0, concat_axis=2, tiled=True)
    return lax.psum_scatter(
        lax.dot_general(
            masked, returned, (((0, 1, 3), (0, 1, 3)), ((), ())), preferred_element_type=jnp.float32
        ),
        "pair",
        scatter_dimension=0,
        tiled=True,
    )


def row_sliced(shape):
    n = shape["pair"]
    return shape["grp"] == 2 and BS % n == 0 and (BS // n) * BS % 128 == 0


def greet(n, me):
    barrier = pltpu.get_barrier_semaphore()

    def hello(k, carry):
        pl.semaphore_signal(
            barrier, inc=1, device_id={"pair": lax.rem(me + k, n)}, device_id_type=MESH
        )
        return carry

    lax.fori_loop(1, n, hello, 0)
    pl.semaphore_signal(
        barrier, inc=1, device_id={"grp": 1 - lax.axis_index("grp")}, device_id_type=MESH
    )
    pl.semaphore_wait(barrier, n)


def swap_major(chunks):
    return jnp.swapaxes(jnp.stack(chunks, axis=0), 0, 1)


def left_chunk(green_ref, tensor_ref, left_ref, rows_at, count):
    half = count // 2
    pairs = BS * BS // 128
    at = pl.ds(rows_at, count)
    low = lax.broadcasted_iota(jnp.int32, (half, pairs, 128), 2) < BS
    rows = []
    for a in range(KN):
        x = swap_major([tensor_ref[a, at, 128 * t : 128 * (t + 1)] for t in range(pairs)])
        first, second = x[:half], x[half:]
        even = jnp.where(low, first, pltpu.roll(second, BS, 2))
        odd = jnp.where(low, pltpu.roll(first, BS, 2), second)
        for y in (even, odd):
            rows.append(jnp.concatenate([y[p] for p in range(half)], axis=1))
    stacked = jnp.concatenate(rows, axis=0)
    result = jnp.dot(green_ref[...], stacked, preferred_element_type=jnp.float32)
    result = result.astype(jnp.bfloat16)
    for a in range(KN):
        base = a * BS
        even = jnp.stack(
            [result[base : base + pairs, 128 * p : 128 * (p + 1)] for p in range(half)], axis=0
        )
        odd = jnp.stack(
            [result[base + pairs : base + BS, 128 * p : 128 * (p + 1)] for p in range(half)],
            axis=0,
        )
        first = jnp.where(low, even, pltpu.roll(odd, BS, 2))
        second = jnp.where(low, pltpu.roll(even, BS, 2), odd)
        back = jnp.swapaxes(jnp.concatenate([first, second], axis=0), 0, 1)
        for t in range(pairs):
            left_ref[a, at, 128 * t : 128 * (t + 1)] = back[t]


def fill_green(n, column, slots_ref, every_ref, green_ref):
    keep_row = KG * BS
    own = slots_ref[column]
    keeps = every_ref[own, keep_row : keep_row + 16, :][:1].astype(jnp.float32)
    for target in range(-HB, HB + 1):
        line = []
        for source in range(-HB, HB + 1):
            step = target - source
            if abs(step) <= HG:
                slot = slots_ref[lax.rem(column + source + n, n)]
                at = (step + HG) * BS
                block = every_ref[slot, at : at + BS, :][:, :BS].astype(jnp.float32)
                keep = keeps[:, source + HB : source + HB + 1]
                line.append((block * keep).astype(jnp.bfloat16))
            else:
                line.append(jnp.zeros((BS, BS), jnp.bfloat16))
        at = (target + HB) * BS
        green_ref[at : at + BS, :] = jnp.concatenate(line, axis=1)


def fill_virt(slot, c, every_ref, virt_ref, which):
    width = virt_ref.shape[1]
    rows = width // BS
    line = lax.broadcasted_iota(jnp.int32, (width, width), 0) // BS
    column = lax.broadcasted_iota(jnp.int32, (width, width), 1) // BS
    at = (c + HG) * BS
    block = every_ref[slot, at : at + BS, :][:, BS : 2 * BS]
    block = jnp.concatenate([block] * rows, axis=1)
    block = jnp.concatenate([block] * rows, axis=0)
    virt_ref[which] = jnp.where(line == column, block, jnp.zeros_like(block))


def add_lanes(at, keeps, here, after, left, left_after, virt, part):
    def times(value, which):
        return jnp.dot(value, virt[which], preferred_element_type=jnp.float32)

    def against(tensor, right):
        return lax.dot_general(
            tensor, right, (((1,), (1,)), ((), ())), preferred_element_type=jnp.float32
        )

    total = part[...]
    for a in range(-HB, HB + 1):
        mid = left[a + HB, :, at]
        right = times(mid, 0)
        if a >= 0:
            right = right + times(left_after[a - 1 + HB, :, at], 1)
        right = (right * keeps[0][:, a + HB : a + HB + 1]).astype(jnp.bfloat16)
        total = total + against(here[a + HB, :, at], right)
        if a >= 0:
            right = times(mid, 2) * keeps[1][:, a - 1 + HB : a + HB]
            total = total + against(after[a - 1 + HB, :, at], right.astype(jnp.bfloat16))
    part[...] = total


def whole_kernel(
    n, chunk, blocks_ref, slots_ref, pack_ref, tensor_ref, out_ref,
    every, green, green_after, virt, left, left_after, rolled, tensor_rows, staged, part, landed,
    pack_send, pack_recv, tensor_send, tensor_recv, back_send, back_recv, pass_send, pass_recv,
    chi_send, chi_recv, own_sem,
):
    me = lax.axis_index("pair")
    grp = lax.axis_index("grp")
    aux = tensor_ref.shape[2]
    width = tensor_rows.shape[3]
    chunks = aux // chunk
    out_rows = aux // n
    half = aux // 2
    share = pl.ds(pl.multiple_of(grp * half, half), half)

    def lanes(to):
        return pl.ds(pl.multiple_of(to * width, width), width)

    def remote(src, dst, send, recv, target):
        return pltpu.make_async_remote_copy(
            src_ref=src, dst_ref=dst, send_sem=send, recv_sem=recv,
            device_id=target, device_id_type=MESH,
        )

    def pack_copy(k):
        to = lax.rem(me + k, n)
        return remote(pack_ref, every.at[me], pack_send.at[k], pack_recv.at[k], {"pair": to})

    def tensor_copy(k):
        to = lax.rem(me + k, n)
        return remote(
            tensor_ref.at[0, :, share, lanes(to)], tensor_rows.at[me],
            tensor_send.at[k], tensor_recv.at[k], {"pair": to},
        )

    def back_copy(k):
        to = lax.rem(me + k, n)
        return remote(
            staged.at[to], rolled.at[:, share, lanes(me)],
            back_send.at[k], back_recv.at[k], {"pair": to},
        )

    def pass_copy(k):
        where = rolled.at[:, share, lanes(lax.rem(me - k + n, n))]
        return remote(where, where, pass_send.at[k], pass_recv.at[k], {"grp": 1 - grp})

    def chi_copy(k):
        to = lax.rem(me + k, n)
        return remote(
            part.at[pl.ds(pl.multiple_of(to * out_rows, out_rows), out_rows)], landed.at[k],
            chi_send.at[k], chi_recv.at[k], {"pair": to},
        )

    def each(act, low=1, high=n):
        def body(k, carry):
            act(k)
            return carry

        lax.fori_loop(low, high, body, 0)

    greet(n, me)
    each(lambda k: pack_copy(k).start())
    each(lambda k: tensor_copy(k).start())
    own_pack = pltpu.make_async_copy(pack_ref, every.at[me], own_sem.at[0])
    own_tensor = pltpu.make_async_copy(
        tensor_ref.at[0, :, share, lanes(me)], tensor_rows.at[me], own_sem.at[1]
    )
    own_pack.start()
    own_tensor.start()
    own_pack.wait()
    each(lambda k: pack_copy(k).wait_recv())
    column = blocks_ref[me]
    column_after = lax.rem(column + 1, n)
    slot, slot_after = slots_ref[column], slots_ref[column_after]
    fill_green(n, column, slots_ref, every, green)
    fill_green(n, column_after, slots_ref, every, green_after)
    fill_virt(slot, 0, every, virt, 0)
    fill_virt(slot, 1, every, virt, 1)
    fill_virt(slot_after, -1, every, virt, 2)

    def own_left(q):
        left_chunk(green, tensor_ref.at[0], left, pl.multiple_of(q * chunk, chunk), chunk)

    each(own_left, 0, chunks)
    own_tensor.wait()
    each(lambda k: tensor_copy(k).wait_recv())

    def stage(k):
        to = lax.rem(me + k, n)
        wanted = slots_ref[lax.rem(blocks_ref[to] + 1, n)]
        for a in range(KN):
            staged[to, a] = tensor_rows[wanted, a]

    def stage_and_send(k):
        stage(k)
        back_copy(k).start()

    each(stage_and_send)
    stage(0)
    own_back = pltpu.make_async_copy(
        staged.at[me], rolled.at[:, share, lanes(me)], own_sem.at[2]
    )
    own_back.start()
    own_back.wait()
    pass_copy(0).start()

    def hand_on(k):
        back_copy(k).wait_recv()
        pass_copy(k).start()

    each(hand_on)

    def after_left(base):
        def act(q):
            at = pl.multiple_of(base + q * chunk, chunk)
            left_chunk(green_after, rolled, left_after, at, chunk)

        each(act, 0, chunks // 2)

    after_left(grp * half)
    each(lambda k: pass_copy(k).wait_recv(), 0)
    after_left((1 - grp) * half)
    part[...] = jnp.zeros_like(part)
    keeps = [
        every[s, KG * BS : KG * BS + 16, :][:1].astype(jnp.float32) for s in (slot, slot_after)
    ]

    def add(t):
        at = pl.ds(pl.multiple_of(t * virt.shape[1], virt.shape[1]), virt.shape[1])
        add_lanes(at, keeps, tensor_ref.at[0], rolled, left, left_after, virt, part)

    each(add, 0, left.shape[2] // virt.shape[1])
    each(lambda k: chi_copy(k).start())

    def sent(k):
        pack_copy(k).wait_send()
        tensor_copy(k).wait_send()
        back_copy(k).wait_send()

    each(sent)
    each(lambda k: pass_copy(k).wait_send(), 0)
    each(lambda k: chi_copy(k).wait_recv())
    total = part[pl.ds(pl.multiple_of(me * out_rows, out_rows), out_rows), :]
    for k in range(1, n):
        total = total + landed[k]
    out_ref[...] = total
    each(lambda k: chi_copy(k).wait_send())


def by_row_slices(three_center, block_mask, green_occ, green_virt, green_mask, block_of_slot):
    n = lax.axis_size("pair")
    aux = three_center.shape[2]
    width = BS * BS // n
    chunk = 32
    slot_of_block = invert(block_of_slot)
    keep = green_mask.astype(jnp.bfloat16)[0, :, None, None]
    occ = green_occ.reshape(KG, BS // 2, 2, BS // 2, 2).transpose(0, 2, 1, 4, 3)
    occ = occ.reshape(KG, BS, BS)
    virt = green_virt.reshape(KG, BS, BS)
    greens = (jnp.concatenate([occ, virt], axis=2) * keep).reshape(KG * BS, 2 * BS)
    mask = jnp.pad(block_mask.astype(jnp.bfloat16), ((0, 15), (0, 2 * BS - KN)))
    pack = jnp.concatenate([greens, mask], axis=0)
    smem = pl.BlockSpec(memory_space=pltpu.SMEM)
    vmem = pl.BlockSpec(memory_space=pltpu.VMEM)
    sems = pltpu.SemaphoreType.DMA
    return pl.pallas_call(
        functools.partial(whole_kernel, n, chunk),
        out_shape=jax.ShapeDtypeStruct((aux // n, aux), jnp.float32),
        in_specs=[smem, smem, vmem, vmem],
        out_specs=vmem,
        scratch_shapes=[
            pltpu.VMEM((n,) + pack.shape, jnp.bfloat16),
            pltpu.VMEM((KN * BS, KN * BS), jnp.bfloat16),
            pltpu.VMEM((KN * BS, KN * BS), jnp.bfloat16),
            pltpu.VMEM((3, 4 * BS, 4 * BS), jnp.bfloat16),
            pltpu.VMEM((KN, aux, BS * BS), jnp.bfloat16),
            pltpu.VMEM((KN, aux, BS * BS), jnp.bfloat16),
            pltpu.VMEM((KN, aux, BS * BS), jnp.bfloat16),
            pltpu.VMEM((n, KN, aux // 2, width), jnp.bfloat16),
            pltpu.VMEM((n, KN, aux // 2, width), jnp.bfloat16),
            pltpu.VMEM((aux, aux), jnp.float32),
            pltpu.VMEM((n, aux // n, aux), jnp.float32),
        ]
        + [sems((n,))] * 10
        + [
            sems((3,)),
        ],
        compiler_params=pltpu.CompilerParams(
            collective_id=0, has_side_effects=True, vmem_limit_bytes=48 * 1024 * 1024
        ),
        name="polarizability",
    )(block_of_slot, slot_of_block, pack, three_center)


def solution(mesh):
    return jax.shard_map(
        by_row_slices if row_sliced(mesh.shape) else on_device,
        mesh=mesh,
        in_specs=(
            P("pair", None, None, None),
            P("pair", None),
            P("pair", "grp", None),
            P("pair", "grp", None),
            P("pair", None),
            P(),
        ),
        out_specs=P("pair", "grp"),
        check_vma=False,
    )
```

```python
import functools

import jax
import jax.numpy as jnp
from jax import lax
from jax.experimental import pallas as pl
from jax.experimental.pallas import tpu as pltpu
from jax.sharding import PartitionSpec as P

BS = 64
HB = 1
HG = 1
KN = 3
KG = 3
MESH = pl.DeviceIdType.MESH


def invert(block_of_slot):
    amount = block_of_slot.shape[0]
    return (
        jnp.zeros((amount,), jnp.int32).at[block_of_slot].set(jnp.arange(amount, dtype=jnp.int32))
    )


def build_left(blocks, columns, gocc, block_count):
    lefts = []
    for target in range(-HB, HB + 1):
        middles = [m for m in range(HG, -HG - 1, -1) if abs(target - m) <= HB]
        green_cat = jnp.concatenate(
            [gocc[(columns + (target - m)) % block_count, m + HG] for m in middles], axis=2
        )
        lowest = target - middles[0] + HB
        tensor_cat = blocks[:, lowest : lowest + len(middles)]
        tensor_cat = tensor_cat.reshape(blocks.shape[0], len(middles) * BS, blocks.shape[3])
        lefts.append(
            jnp.einsum(
                "lij,ljq->liq", green_cat, tensor_cat, preferred_element_type=jnp.float32
            ).astype(jnp.bfloat16)
        )
    return jnp.stack(lefts, axis=1)


def build_right(left_turned, gvirt):
    rights = []
    count = left_turned.shape[0]
    for target in range(-HB, HB + 1):
        middles = [m for m in range(-HG, HG + 1) if abs(target - m) <= HB]
        virt_cat = gvirt[:, middles[0] + HG : middles[-1] + HG + 1].reshape(
            count, len(middles) * BS, BS
        )
        left_cat = jnp.concatenate(
            [jnp.roll(left_turned[:, target - m + HB], -m, axis=0) for m in middles], axis=1
        )
        rights.append(
            jnp.einsum(
                "ljk,ljq->lkq", virt_cat, left_cat, preferred_element_type=jnp.float32
            ).astype(jnp.bfloat16)
        )
    return jnp.stack(rights, axis=1)


def on_device(three_center, block_mask, green_occ, green_virt, green_mask, block_of_slot):
    aux_count = three_center.shape[2]
    block_count = block_of_slot.shape[0]
    local_aux = aux_count // lax.axis_size("pair")
    slot_of_block = invert(block_of_slot)
    masked = three_center * block_mask.astype(jnp.bfloat16)[:, :, None, None]
    green_keep = green_mask.astype(jnp.bfloat16)[:, :, None]
    every_occ, every_virt = (
        lax.all_gather(green_occ * green_keep, "pair", axis=0, tiled=True),
        lax.all_gather(green_virt * green_keep, "pair", axis=0, tiled=True),
    )
    gocc = every_occ[slot_of_block].reshape(block_count, KG, BS, BS)
    gvirt = every_virt[slot_of_block].reshape(block_count, KG, BS, BS)
    regrouped = lax.all_to_all(masked, "pair", split_axis=2, concat_axis=0, tiled=True)
    curve = regrouped[slot_of_block].reshape(block_count, KN, local_aux, BS, BS)
    curve = curve.transpose(0, 1, 3, 2, 4).reshape(block_count, KN, BS, local_aux * BS)
    left = build_left(curve, jnp.arange(block_count, dtype=jnp.int32), gocc, block_count)
    left = left.reshape(block_count, KN, BS, local_aux, BS)
    left_turned = left.transpose(0, 1, 4, 3, 2).reshape(block_count, KN, BS, local_aux * BS)
    right_turned = build_right(left_turned, gvirt)
    right = right_turned.reshape(block_count, KN, BS, local_aux, BS).transpose(0, 1, 3, 4, 2)
    right_slots = right.reshape(block_count, KN, local_aux, BS * BS)[block_of_slot]
    returned = lax.all_to_all(right_slots, "pair", split_axis=0, concat_axis=2, tiled=True)
    return lax.psum_scatter(
        lax.dot_general(
            masked, returned, (((0, 1, 3), (0, 1, 3)), ((), ())), preferred_element_type=jnp.float32
        ),
        "pair",
        scatter_dimension=0,
        tiled=True,
    )


def row_sliced(shape):
    n = shape["pair"]
    return shape["grp"] == 2 and BS % n == 0 and (BS // n) * BS % 128 == 0


def greet(n, me):
    barrier = pltpu.get_barrier_semaphore()

    def hello(k, carry):
        pl.semaphore_signal(
            barrier, inc=1, device_id={"pair": lax.rem(me + k, n)}, device_id_type=MESH
        )
        return carry

    lax.fori_loop(1, n, hello, 0)
    pl.semaphore_signal(
        barrier, inc=1, device_id={"grp": 1 - lax.axis_index("grp")}, device_id_type=MESH
    )
    pl.semaphore_wait(barrier, n)


def swap_major(chunks):
    return jnp.swapaxes(jnp.stack(chunks, axis=0), 0, 1)


def left_chunk(green_ref, tensor_ref, left_ref, rows_at, count):
    half = count // 2
    pairs = BS * BS // 128
    at = pl.ds(rows_at, count)
    low = lax.broadcasted_iota(jnp.int32, (half, pairs, 128), 2) < BS
    rows = []
    for a in range(KN):
        x = swap_major([tensor_ref[a, at, 128 * t : 128 * (t + 1)] for t in range(pairs)])
        first, second = x[:half], x[half:]
        even = jnp.where(low, first, pltpu.roll(second, BS, 2))
        odd = jnp.where(low, pltpu.roll(first, BS, 2), second)
        for y in (even, odd):
            rows.append(jnp.concatenate([y[p] for p in range(half)], axis=1))
    stacked = jnp.concatenate(rows, axis=0)
    result = jnp.dot(green_ref[...], stacked, preferred_element_type=jnp.float32)
    result = result.astype(jnp.bfloat16)
    for a in range(KN):
        base = a * BS
        even = jnp.stack(
            [result[base : base + pairs, 128 * p : 128 * (p + 1)] for p in range(half)], axis=0
        )
        odd = jnp.stack(
            [result[base + pairs : base + BS, 128 * p : 128 * (p + 1)] for p in range(half)],
            axis=0,
        )
        first = jnp.where(low, even, pltpu.roll(odd, BS, 2))
        second = jnp.where(low, pltpu.roll(even, BS, 2), odd)
        back = jnp.swapaxes(jnp.concatenate([first, second], axis=0), 0, 1)
        for t in range(pairs):
            left_ref[a, at, 128 * t : 128 * (t + 1)] = back[t]


def fill_green(n, column, slots_ref, every_ref, green_ref):
    keep_row = KG * BS
    own = slots_ref[column]
    keeps = every_ref[own, keep_row : keep_row + 16, :][:1].astype(jnp.float32)
    for target in range(-HB, HB + 1):
        line = []
        for source in range(-HB, HB + 1):
            step = target - source
            if abs(step) <= HG:
                slot = slots_ref[lax.rem(column + source + n, n)]
                at = (step + HG) * BS
                block = every_ref[slot, at : at + BS, :][:, :BS].astype(jnp.float32)
                keep = keeps[:, source + HB : source + HB + 1]
                line.append((block * keep).astype(jnp.bfloat16))
            else:
                line.append(jnp.zeros((BS, BS), jnp.bfloat16))
        at = (target + HB) * BS
        green_ref[at : at + BS, :] = jnp.concatenate(line, axis=1)


def fill_virt(slot, c, every_ref, virt_ref, which):
    width = virt_ref.shape[1]
    rows = width // BS
    line = lax.broadcasted_iota(jnp.int32, (width, width), 0) // BS
    column = lax.broadcasted_iota(jnp.int32, (width, width), 1) // BS
    at = (c + HG) * BS
    block = every_ref[slot, at : at + BS, :][:, BS : 2 * BS]
    block = jnp.concatenate([block] * rows, axis=1)
    block = jnp.concatenate([block] * rows, axis=0)
    virt_ref[which] = jnp.where(line == column, block, jnp.zeros_like(block))


def add_lanes(at, keeps, here, after, left, left_after, virt, part):
    def times(value, which):
        return jnp.dot(value, virt[which], preferred_element_type=jnp.float32)

    def against(tensor, right):
        return lax.dot_general(
            tensor, right, (((1,), (1,)), ((), ())), preferred_element_type=jnp.float32
        )

    total = part[...]
    for a in range(-HB, HB + 1):
        mid = left[a + HB, :, at]
        right = times(mid, 0)
        if a >= 0:
            right = right + times(left_after[a - 1 + HB, :, at], 1)
        right = (right * keeps[0][:, a + HB : a + HB + 1]).astype(jnp.bfloat16)
        total = total + against(here[a + HB, :, at], right)
        if a >= 0:
            right = times(mid, 2) * keeps[1][:, a - 1 + HB : a + HB]
            total = total + against(after[a - 1 + HB, :, at], right.astype(jnp.bfloat16))
    part[...] = total


def whole_kernel(
    n, chunk, blocks_ref, slots_ref, pack_ref, tensor_ref, out_ref,
    every, green, green_after, virt, left, left_after, rolled, part, landed,
    pack_send, pack_recv, tensor_send, tensor_recv, back_send, back_recv, pass_send, pass_recv,
    chi_send, chi_recv, own_sem, own_tensor_sem, own_back_sem, *buffers,
):
    me = lax.axis_index("pair")
    grp = lax.axis_index("grp")
    aux = tensor_ref.shape[2]
    pieces = len(buffers) // 2
    tensor_rows, staged = buffers[:pieces], buffers[pieces:]
    piece = aux // 2 // pieces
    width = tensor_rows[0].shape[3]
    chunks = aux // chunk
    out_rows = aux // n
    half = aux // 2

    def share(p):
        return pl.ds(pl.multiple_of(grp * half + p * piece, piece), piece)

    def lanes(to):
        return pl.ds(pl.multiple_of(to * width, width), width)

    def remote(src, dst, send, recv, target):
        return pltpu.make_async_remote_copy(
            src_ref=src, dst_ref=dst, send_sem=send, recv_sem=recv,
            device_id=target, device_id_type=MESH,
        )

    def pack_copy(k):
        to = lax.rem(me + k, n)
        return remote(pack_ref, every.at[me], pack_send.at[k], pack_recv.at[k], {"pair": to})

    def tensor_copy(p, k):
        to = lax.rem(me + k, n)
        return remote(
            tensor_ref.at[0, :, share(p), lanes(to)], tensor_rows[p].at[me],
            tensor_send.at[p, k], tensor_recv.at[p, k], {"pair": to},
        )

    def back_copy(p, k):
        to = lax.rem(me + k, n)
        return remote(
            staged[p].at[to], rolled.at[:, share(p), lanes(me)],
            back_send.at[p, k], back_recv.at[p, k], {"pair": to},
        )

    def pass_copy(p, k):
        where = rolled.at[:, share(p), lanes(lax.rem(me - k + n, n))]
        return remote(where, where, pass_send.at[p, k], pass_recv.at[p, k], {"grp": 1 - grp})

    def chi_copy(k):
        to = lax.rem(me + k, n)
        return remote(
            part.at[pl.ds(pl.multiple_of(to * out_rows, out_rows), out_rows)], landed.at[k],
            chi_send.at[k], chi_recv.at[k], {"pair": to},
        )

    def each(act, low=1, high=n):
        def body(k, carry):
            act(k)
            return carry

        lax.fori_loop(low, high, body, 0)

    def own_tensor(p):
        return pltpu.make_async_copy(
            tensor_ref.at[0, :, share(p), lanes(me)], tensor_rows[p].at[me], own_tensor_sem.at[p]
        )

    def own_back(p):
        return pltpu.make_async_copy(
            staged[p].at[me], rolled.at[:, share(p), lanes(me)], own_back_sem.at[p]
        )

    def stage(p, k):
        to = lax.rem(me + k, n)
        wanted = slots_ref[lax.rem(blocks_ref[to] + 1, n)]
        for a in range(KN):
            staged[p][to, a] = tensor_rows[p][wanted, a]

    def stage_and_send(p, k):
        stage(p, k)
        back_copy(p, k).start()

    def own_left(q):
        left_chunk(green, tensor_ref.at[0], left, pl.multiple_of(q * chunk, chunk), chunk)

    def hand_on(p, k):
        back_copy(p, k).wait_recv()
        pass_copy(p, k).start()

    def after_left(base):
        def act(q):
            at = pl.multiple_of(base + q * chunk, chunk)
            left_chunk(green_after, rolled, left_after, at, chunk)

        each(act, 0, piece // chunk)

    greet(n, me)
    each(lambda k: pack_copy(k).start())
    for p in range(pieces):
        each(lambda k: tensor_copy(p, k).start())
        own_tensor(p).start()
    own_pack = pltpu.make_async_copy(pack_ref, every.at[me], own_sem.at[0])
    own_pack.start()
    own_pack.wait()
    each(lambda k: pack_copy(k).wait_recv())
    column = blocks_ref[me]
    column_after = lax.rem(column + 1, n)
    slot, slot_after = slots_ref[column], slots_ref[column_after]
    fill_green(n, column, slots_ref, every, green)
    fill_green(n, column_after, slots_ref, every, green_after)
    fill_virt(slot, 0, every, virt, 0)
    fill_virt(slot, 1, every, virt, 1)
    fill_virt(slot_after, -1, every, virt, 2)
    per_piece = chunks // pieces
    for p in range(pieces):
        own_tensor(p).wait()
        each(lambda k: tensor_copy(p, k).wait_recv())
        each(lambda k: stage_and_send(p, k))
        stage(p, 0)
        own_back(p).start()
        each(own_left, p * per_piece, (p + 1) * per_piece)
    for p in range(pieces):
        own_back(p).wait()
        pass_copy(p, 0).start()
        each(lambda k: hand_on(p, k))
        after_left(grp * half + p * piece)
    for p in range(pieces):
        each(lambda k: pass_copy(p, k).wait_recv(), 0)
        after_left((1 - grp) * half + p * piece)
    part[...] = jnp.zeros_like(part)
    keeps = [
        every[s, KG * BS : KG * BS + 16, :][:1].astype(jnp.float32) for s in (slot, slot_after)
    ]

    def add(t):
        at = pl.ds(pl.multiple_of(t * virt.shape[1], virt.shape[1]), virt.shape[1])
        add_lanes(at, keeps, tensor_ref.at[0], rolled, left, left_after, virt, part)

    each(add, 0, left.shape[2] // virt.shape[1])
    each(lambda k: chi_copy(k).start())

    def sent(k):
        pack_copy(k).wait_send()
        for p in range(pieces):
            tensor_copy(p, k).wait_send()
            back_copy(p, k).wait_send()

    each(sent)
    for p in range(pieces):
        each(lambda k: pass_copy(p, k).wait_send(), 0)
    each(lambda k: chi_copy(k).wait_recv())
    total = part[pl.ds(pl.multiple_of(me * out_rows, out_rows), out_rows), :]
    for k in range(1, n):
        total = total + landed[k]
    out_ref[...] = total
    each(lambda k: chi_copy(k).wait_send())


def by_row_slices(three_center, block_mask, green_occ, green_virt, green_mask, block_of_slot):
    n = lax.axis_size("pair")
    aux = three_center.shape[2]
    width = BS * BS // n
    chunk = 32
    pieces = 4
    slot_of_block = invert(block_of_slot)
    keep = green_mask.astype(jnp.bfloat16)[0, :, None, None]
    occ = green_occ.reshape(KG, BS // 2, 2, BS // 2, 2).transpose(0, 2, 1, 4, 3)
    occ = occ.reshape(KG, BS, BS)
    virt = green_virt.reshape(KG, BS, BS)
    greens = (jnp.concatenate([occ, virt], axis=2) * keep).reshape(KG * BS, 2 * BS)
    mask = jnp.pad(block_mask.astype(jnp.bfloat16), ((0, 15), (0, 2 * BS - KN)))
    pack = jnp.concatenate([greens, mask], axis=0)
    smem = pl.BlockSpec(memory_space=pltpu.SMEM)
    vmem = pl.BlockSpec(memory_space=pltpu.VMEM)
    sems = pltpu.SemaphoreType.DMA
    return pl.pallas_call(
        functools.partial(whole_kernel, n, chunk),
        out_shape=jax.ShapeDtypeStruct((aux // n, aux), jnp.float32),
        in_specs=[smem, smem, vmem, vmem],
        out_specs=vmem,
        scratch_shapes=[
            pltpu.VMEM((n,) + pack.shape, jnp.bfloat16),
            pltpu.VMEM((KN * BS, KN * BS), jnp.bfloat16),
            pltpu.VMEM((KN * BS, KN * BS), jnp.bfloat16),
            pltpu.VMEM((3, 4 * BS, 4 * BS), jnp.bfloat16),
            pltpu.VMEM((KN, aux, BS * BS), jnp.bfloat16),
            pltpu.VMEM((KN, aux, BS * BS), jnp.bfloat16),
            pltpu.VMEM((KN, aux, BS * BS), jnp.bfloat16),
            pltpu.VMEM((aux, aux), jnp.float32),
            pltpu.VMEM((n, aux // n, aux), jnp.float32),
        ]
        + [sems((n,))] * 2
        + [sems((pieces, n))] * 6
        + [sems((n,))] * 2
        + [sems((1,)), sems((pieces,)), sems((pieces,))]
        + [pltpu.VMEM((n, KN, aux // 2 // pieces, width), jnp.bfloat16)] * (2 * pieces),
        compiler_params=pltpu.CompilerParams(
            collective_id=0, has_side_effects=True, vmem_limit_bytes=48 * 1024 * 1024
        ),
        name="polarizability",
    )(block_of_slot, slot_of_block, pack, three_center)


def solution(mesh):
    return jax.shard_map(
        by_row_slices if row_sliced(mesh.shape) else on_device,
        mesh=mesh,
        in_specs=(
            P("pair", None, None, None),
            P("pair", None),
            P("pair", "grp", None),
            P("pair", "grp", None),
            P("pair", None),
            P(),
        ),
        out_specs=P("pair", "grp"),
        check_vma=False,
    )
```

```python
import functools

import jax
import jax.numpy as jnp
from jax import lax
from jax.experimental import pallas as pl
from jax.experimental.pallas import tpu as pltpu
from jax.sharding import PartitionSpec as P

BS = 64
HB = 1
HG = 1
KN = 3
KG = 3
MESH = pl.DeviceIdType.MESH


def invert(block_of_slot):
    amount = block_of_slot.shape[0]
    return (
        jnp.zeros((amount,), jnp.int32).at[block_of_slot].set(jnp.arange(amount, dtype=jnp.int32))
    )


def build_left(blocks, columns, gocc, block_count):
    lefts = []
    for target in range(-HB, HB + 1):
        middles = [m for m in range(HG, -HG - 1, -1) if abs(target - m) <= HB]
        green_cat = jnp.concatenate(
            [gocc[(columns + (target - m)) % block_count, m + HG] for m in middles], axis=2
        )
        lowest = target - middles[0] + HB
        tensor_cat = blocks[:, lowest : lowest + len(middles)]
        tensor_cat = tensor_cat.reshape(blocks.shape[0], len(middles) * BS, blocks.shape[3])
        lefts.append(
            jnp.einsum(
                "lij,ljq->liq", green_cat, tensor_cat, preferred_element_type=jnp.float32
            ).astype(jnp.bfloat16)
        )
    return jnp.stack(lefts, axis=1)


def build_right(left_turned, gvirt):
    rights = []
    count = left_turned.shape[0]
    for target in range(-HB, HB + 1):
        middles = [m for m in range(-HG, HG + 1) if abs(target - m) <= HB]
        virt_cat = gvirt[:, middles[0] + HG : middles[-1] + HG + 1].reshape(
            count, len(middles) * BS, BS
        )
        left_cat = jnp.concatenate(
            [jnp.roll(left_turned[:, target - m + HB], -m, axis=0) for m in middles], axis=1
        )
        rights.append(
            jnp.einsum(
                "ljk,ljq->lkq", virt_cat, left_cat, preferred_element_type=jnp.float32
            ).astype(jnp.bfloat16)
        )
    return jnp.stack(rights, axis=1)


def on_device(three_center, block_mask, green_occ, green_virt, green_mask, block_of_slot):
    aux_count = three_center.shape[2]
    block_count = block_of_slot.shape[0]
    local_aux = aux_count // lax.axis_size("pair")
    slot_of_block = invert(block_of_slot)
    masked = three_center * block_mask.astype(jnp.bfloat16)[:, :, None, None]
    green_keep = green_mask.astype(jnp.bfloat16)[:, :, None]
    every_occ, every_virt = (
        lax.all_gather(green_occ * green_keep, "pair", axis=0, tiled=True),
        lax.all_gather(green_virt * green_keep, "pair", axis=0, tiled=True),
    )
    gocc = every_occ[slot_of_block].reshape(block_count, KG, BS, BS)
    gvirt = every_virt[slot_of_block].reshape(block_count, KG, BS, BS)
    regrouped = lax.all_to_all(masked, "pair", split_axis=2, concat_axis=0, tiled=True)
    curve = regrouped[slot_of_block].reshape(block_count, KN, local_aux, BS, BS)
    curve = curve.transpose(0, 1, 3, 2, 4).reshape(block_count, KN, BS, local_aux * BS)
    left = build_left(curve, jnp.arange(block_count, dtype=jnp.int32), gocc, block_count)
    left = left.reshape(block_count, KN, BS, local_aux, BS)
    left_turned = left.transpose(0, 1, 4, 3, 2).reshape(block_count, KN, BS, local_aux * BS)
    right_turned = build_right(left_turned, gvirt)
    right = right_turned.reshape(block_count, KN, BS, local_aux, BS).transpose(0, 1, 3, 4, 2)
    right_slots = right.reshape(block_count, KN, local_aux, BS * BS)[block_of_slot]
    returned = lax.all_to_all(right_slots, "pair", split_axis=0, concat_axis=2, tiled=True)
    return lax.psum_scatter(
        lax.dot_general(
            masked, returned, (((0, 1, 3), (0, 1, 3)), ((), ())), preferred_element_type=jnp.float32
        ),
        "pair",
        scatter_dimension=0,
        tiled=True,
    )


def row_sliced(shape):
    n = shape["pair"]
    return shape["grp"] == 2 and BS % n == 0 and (BS // n) * BS % 128 == 0


def greet(n, me):
    barrier = pltpu.get_barrier_semaphore()

    def hello(k, carry):
        pl.semaphore_signal(
            barrier, inc=1, device_id={"pair": lax.rem(me + k, n)}, device_id_type=MESH
        )
        return carry

    lax.fori_loop(1, n, hello, 0)
    pl.semaphore_signal(
        barrier, inc=1, device_id={"grp": 1 - lax.axis_index("grp")}, device_id_type=MESH
    )
    pl.semaphore_wait(barrier, n)


def swap_major(chunks):
    return jnp.swapaxes(jnp.stack(chunks, axis=0), 0, 1)


def left_chunk(green_ref, tensor_ref, left_ref, rows_at, count):
    half = count // 2
    pairs = BS * BS // 128
    at = pl.ds(rows_at, count)
    low = lax.broadcasted_iota(jnp.int32, (half, pairs, 128), 2) < BS
    rows = []
    for a in range(KN):
        x = swap_major([tensor_ref[a, at, 128 * t : 128 * (t + 1)] for t in range(pairs)])
        first, second = x[:half], x[half:]
        even = jnp.where(low, first, pltpu.roll(second, BS, 2))
        odd = jnp.where(low, pltpu.roll(first, BS, 2), second)
        for y in (even, odd):
            rows.append(jnp.concatenate([y[p] for p in range(half)], axis=1))
    stacked = jnp.concatenate(rows, axis=0)
    result = jnp.dot(green_ref[...], stacked, preferred_element_type=jnp.float32)
    result = result.astype(jnp.bfloat16)
    for a in range(KN):
        base = a * BS
        even = jnp.stack(
            [result[base : base + pairs, 128 * p : 128 * (p + 1)] for p in range(half)], axis=0
        )
        odd = jnp.stack(
            [result[base + pairs : base + BS, 128 * p : 128 * (p + 1)] for p in range(half)],
            axis=0,
        )
        first = jnp.where(low, even, pltpu.roll(odd, BS, 2))
        second = jnp.where(low, pltpu.roll(even, BS, 2), odd)
        back = jnp.swapaxes(jnp.concatenate([first, second], axis=0), 0, 1)
        for t in range(pairs):
            left_ref[a, at, 128 * t : 128 * (t + 1)] = back[t]


def fill_green(n, column, slots_ref, every_ref, green_ref):
    keep_row = KG * BS
    own = slots_ref[column]
    keeps = every_ref[own, keep_row : keep_row + 16, :][:1].astype(jnp.float32)
    for target in range(-HB, HB + 1):
        line = []
        for source in range(-HB, HB + 1):
            step = target - source
            if abs(step) <= HG:
                slot = slots_ref[lax.rem(column + source + n, n)]
                at = (step + HG) * BS
                block = every_ref[slot, at : at + BS, :][:, :BS].astype(jnp.float32)
                keep = keeps[:, source + HB : source + HB + 1]
                line.append((block * keep).astype(jnp.bfloat16))
            else:
                line.append(jnp.zeros((BS, BS), jnp.bfloat16))
        at = (target + HB) * BS
        green_ref[at : at + BS, :] = jnp.concatenate(line, axis=1)


def fill_virt(slot, c, every_ref, virt_ref, which):
    width = virt_ref.shape[1]
    rows = width // BS
    line = lax.broadcasted_iota(jnp.int32, (width, width), 0) // BS
    column = lax.broadcasted_iota(jnp.int32, (width, width), 1) // BS
    at = (c + HG) * BS
    block = every_ref[slot, at : at + BS, :][:, BS : 2 * BS]
    block = jnp.concatenate([block] * rows, axis=1)
    block = jnp.concatenate([block] * rows, axis=0)
    virt_ref[which] = jnp.where(line == column, block, jnp.zeros_like(block))


def add_lanes(at, keeps, here, after, left, left_after, virt, part):
    def times(value, which):
        return jnp.dot(value, virt[which], preferred_element_type=jnp.float32)

    def against(tensor, right):
        return lax.dot_general(
            tensor, right, (((1,), (1,)), ((), ())), preferred_element_type=jnp.float32
        )

    total = part[...]
    for a in range(-HB, HB + 1):
        mid = left[a + HB, :, at]
        right = times(mid, 0)
        if a >= 0:
            right = right + times(left_after[a - 1 + HB, :, at], 1)
        right = (right * keeps[0][:, a + HB : a + HB + 1]).astype(jnp.bfloat16)
        total = total + against(here[a + HB, :, at], right)
        if a >= 0:
            right = times(mid, 2) * keeps[1][:, a - 1 + HB : a + HB]
            total = total + against(after[a - 1 + HB, :, at], right.astype(jnp.bfloat16))
    part[...] = total


def whole_kernel(
    n, chunk, blocks_ref, slots_ref, pack_ref, tensor_ref, out_ref,
    every, green, green_after, virt, left, left_after, rolled, part, landed,
    pack_send, pack_recv, tensor_send, tensor_recv, back_send, back_recv, pass_send, pass_recv,
    chi_send, chi_recv, own_sem, own_tensor_sem, own_back_sem, *buffers,
):
    me = lax.axis_index("pair")
    grp = lax.axis_index("grp")
    aux = tensor_ref.shape[2]
    pieces = len(buffers) // 2
    tensor_rows, staged = buffers[:pieces], buffers[pieces:]
    piece = aux // 2 // pieces
    width = tensor_rows[0].shape[3]
    chunks = aux // chunk
    out_rows = aux // n
    half = aux // 2

    def share(p):
        return pl.ds(pl.multiple_of(grp * half + p * piece, piece), piece)

    def lanes(to):
        return pl.ds(pl.multiple_of(to * width, width), width)

    def remote(src, dst, send, recv, target):
        return pltpu.make_async_remote_copy(
            src_ref=src, dst_ref=dst, send_sem=send, recv_sem=recv,
            device_id=target, device_id_type=MESH,
        )

    def pack_copy(k):
        to = lax.rem(me + k, n)
        return remote(pack_ref, every.at[me], pack_send.at[k], pack_recv.at[k], {"pair": to})

    def tensor_copy(p, k):
        to = lax.rem(me + k, n)
        return remote(
            tensor_ref.at[0, :, share(p), lanes(to)], tensor_rows[p].at[me],
            tensor_send.at[p, k], tensor_recv.at[p, k], {"pair": to},
        )

    def back_copy(p, k):
        to = lax.rem(me + k, n)
        return remote(
            staged[p].at[to], rolled.at[:, share(p), lanes(me)],
            back_send.at[p, k], back_recv.at[p, k], {"pair": to},
        )

    def pass_copy(p, k):
        where = rolled.at[:, share(p), lanes(lax.rem(me - k + n, n))]
        return remote(where, where, pass_send.at[p, k], pass_recv.at[p, k], {"grp": 1 - grp})

    def chi_copy(k):
        to = lax.rem(me + k, n)
        return remote(
            part.at[pl.ds(pl.multiple_of(to * out_rows, out_rows), out_rows)], landed.at[k],
            chi_send.at[k], chi_recv.at[k], {"pair": to},
        )

    def each(act, low=1, high=n):
        def body(k, carry):
            act(k)
            return carry

        lax.fori_loop(low, high, body, 0)

    def own_tensor(p):
        return pltpu.make_async_copy(
            tensor_ref.at[0, :, share(p), lanes(me)], tensor_rows[p].at[me], own_tensor_sem.at[p]
        )

    def own_back(p):
        return pltpu.make_async_copy(
            staged[p].at[me], rolled.at[:, share(p), lanes(me)], own_back_sem.at[p]
        )

    def stage(p, k):
        to = lax.rem(me + k, n)
        wanted = slots_ref[lax.rem(blocks_ref[to] + 1, n)]
        for a in range(KN):
            staged[p][to, a] = tensor_rows[p][wanted, a]

    def stage_and_send(p, k):
        stage(p, k)
        back_copy(p, k).start()

    def own_left(q):
        left_chunk(green, tensor_ref.at[0], left, pl.multiple_of(q * chunk, chunk), chunk)

    def hand_on(p, k):
        back_copy(p, k).wait_recv()
        pass_copy(p, k).start()

    def after_left(base):
        def act(q):
            at = pl.multiple_of(base + q * chunk, chunk)
            left_chunk(green_after, rolled, left_after, at, chunk)

        each(act, 0, piece // chunk)

    def mixed(act):
        each(lambda k: act(lax.rem(7 * k, n)))

    greet(n, me)
    each(lambda k: pack_copy(k).start())
    for p in range(pieces):
        mixed(lambda k: tensor_copy(p, k).start())
        own_tensor(p).start()
    own_pack = pltpu.make_async_copy(pack_ref, every.at[me], own_sem.at[0])
    own_pack.start()
    own_pack.wait()
    each(lambda k: pack_copy(k).wait_recv())
    column = blocks_ref[me]
    column_after = lax.rem(column + 1, n)
    slot, slot_after = slots_ref[column], slots_ref[column_after]
    fill_green(n, column, slots_ref, every, green)
    fill_green(n, column_after, slots_ref, every, green_after)
    fill_virt(slot, 0, every, virt, 0)
    fill_virt(slot, 1, every, virt, 1)
    fill_virt(slot_after, -1, every, virt, 2)
    per_piece = chunks // pieces
    for p in range(pieces):
        own_tensor(p).wait()
        each(lambda k: tensor_copy(p, k).wait_recv())
        mixed(lambda k: stage_and_send(p, k))
        stage(p, 0)
        own_back(p).start()
        each(own_left, p * per_piece, (p + 1) * per_piece)
    for p in range(pieces):
        own_back(p).wait()
        pass_copy(p, 0).start()
        mixed(lambda k: hand_on(p, k))
        after_left(grp * half + p * piece)
    for p in range(pieces):
        each(lambda k: pass_copy(p, k).wait_recv(), 0)
        after_left((1 - grp) * half + p * piece)
    part[...] = jnp.zeros_like(part)
    keeps = [
        every[s, KG * BS : KG * BS + 16, :][:1].astype(jnp.float32) for s in (slot, slot_after)
    ]

    def add(t):
        at = pl.ds(pl.multiple_of(t * virt.shape[1], virt.shape[1]), virt.shape[1])
        add_lanes(at, keeps, tensor_ref.at[0], rolled, left, left_after, virt, part)

    each(add, 0, left.shape[2] // virt.shape[1])
    each(lambda k: chi_copy(k).start())

    def sent(k):
        pack_copy(k).wait_send()
        for p in range(pieces):
            tensor_copy(p, k).wait_send()
            back_copy(p, k).wait_send()

    each(sent)
    for p in range(pieces):
        each(lambda k: pass_copy(p, k).wait_send(), 0)
    each(lambda k: chi_copy(k).wait_recv())
    total = part[pl.ds(pl.multiple_of(me * out_rows, out_rows), out_rows), :]
    for k in range(1, n):
        total = total + landed[k]
    out_ref[...] = total
    each(lambda k: chi_copy(k).wait_send())


def by_row_slices(three_center, block_mask, green_occ, green_virt, green_mask, block_of_slot):
    n = lax.axis_size("pair")
    aux = three_center.shape[2]
    width = BS * BS // n
    chunk = 32
    pieces = 4
    slot_of_block = invert(block_of_slot)
    keep = green_mask.astype(jnp.bfloat16)[0, :, None, None]
    occ = green_occ.reshape(KG, BS // 2, 2, BS // 2, 2).transpose(0, 2, 1, 4, 3)
    occ = occ.reshape(KG, BS, BS)
    virt = green_virt.reshape(KG, BS, BS)
    greens = (jnp.concatenate([occ, virt], axis=2) * keep).reshape(KG * BS, 2 * BS)
    mask = jnp.pad(block_mask.astype(jnp.bfloat16), ((0, 15), (0, 2 * BS - KN)))
    pack = jnp.concatenate([greens, mask], axis=0)
    smem = pl.BlockSpec(memory_space=pltpu.SMEM)
    vmem = pl.BlockSpec(memory_space=pltpu.VMEM)
    sems = pltpu.SemaphoreType.DMA
    return pl.pallas_call(
        functools.partial(whole_kernel, n, chunk),
        out_shape=jax.ShapeDtypeStruct((aux // n, aux), jnp.float32),
        in_specs=[smem, smem, vmem, vmem],
        out_specs=vmem,
        scratch_shapes=[
            pltpu.VMEM((n,) + pack.shape, jnp.bfloat16),
            pltpu.VMEM((KN * BS, KN * BS), jnp.bfloat16),
            pltpu.VMEM((KN * BS, KN * BS), jnp.bfloat16),
            pltpu.VMEM((3, 4 * BS, 4 * BS), jnp.bfloat16),
            pltpu.VMEM((KN, aux, BS * BS), jnp.bfloat16),
            pltpu.VMEM((KN, aux, BS * BS), jnp.bfloat16),
            pltpu.VMEM((KN, aux, BS * BS), jnp.bfloat16),
            pltpu.VMEM((aux, aux), jnp.float32),
            pltpu.VMEM((n, aux // n, aux), jnp.float32),
        ]
        + [sems((n,))] * 2
        + [sems((pieces, n))] * 6
        + [sems((n,))] * 2
        + [sems((1,)), sems((pieces,)), sems((pieces,))]
        + [pltpu.VMEM((n, KN, aux // 2 // pieces, width), jnp.bfloat16)] * (2 * pieces),
        compiler_params=pltpu.CompilerParams(
            collective_id=0, has_side_effects=True, vmem_limit_bytes=48 * 1024 * 1024
        ),
        name="polarizability",
    )(block_of_slot, slot_of_block, pack, three_center)


def solution(mesh):
    return jax.shard_map(
        by_row_slices if row_sliced(mesh.shape) else on_device,
        mesh=mesh,
        in_specs=(
            P("pair", None, None, None),
            P("pair", None),
            P("pair", "grp", None),
            P("pair", "grp", None),
            P("pair", None),
            P(),
        ),
        out_specs=P("pair", "grp"),
        check_vma=False,
    )
```
